512 devices in a mesh: blk: 64 (over x, z), span: 8 (over y, core).
Axes of the slice: x: 4, y: 4, z: 16, core: 2. Of those that a mesh axis runs over, the one named last changes fastest.
Arguments:
- fields: float32 [5, 6, 6, 6, 131072], P(None, None, None, None, ('blk', 'span')), may hold values from -6 to 6
- jacobian: float32 [131072], P(('blk', 'span')), may hold values from 0.5 to 2
- mean_flow: float32 [3], replicated, may hold values from -0.5 to 0.5
- pair_owner: int32 [65536, 1], P(('blk', 'span')), may hold values from 0 to 63, as said below
- pair_mortar: int32 [65536], P(('blk', 'span')), may hold values from 0 to 63
- mortar_proj: float32 [2, 2, 6, 6], replicated, may hold values from -2.5 to 2.5
- coarse_id: int32 [131072], P(('blk', 'span')), may hold values from 0 to 255
Outputs:
- new_fields: float32 [5, 6, 6, 6, 131072], P(None, None, None, None, ('blk', 'span'))
- coarse_residual: float32 [40, 16384], P(None, ('blk', 'span'))
The draws below stay inside these ranges and needn't reach their ends.
Inputs may be any that keep to these rules, and one draw needn't show every extreme that they name: `pair_owner`: the owner of every pair of a device with blk index b is b - 1, b or b + 1 modulo 64; among the 128 pairs of one device at most 64 name the same owner, and in every draw some owner is named by exactly 64 of them.
All inputs are finite; a program needn't handle non-finite values.
Results may differ from the reference program's by a relative error of at most 0.0003.
Values sent between devices are 32-bit elements; how exact they have to be, the bound alone decides.
No kernel may reach another device: no remote copies, remote signals or barrier semaphores. Data moves between devices by JAX's collectives and lax.ppermute only.
A program may use at most 128 MiB of HBM per device.

```python
import math
import jax
import jax.numpy as jnp
import numpy as np
from jax import lax

NP = 6
NV = 5
E_DEV = 256
FS_DEV = 64
PAIRS_DEV = 128
CAP = 64
ELEMS = 131072
PAIRS = 65536
AGG_BLK = 256
AGGS = 16384
N_BLK = 64
N_SPAN = 8
DEVICES = 512


def permute_block(block_key):
    return jax.random.permutation(block_key, PAIRS_DEV)


def draw_pair_owner(key, part):
    key = jax.random.fold_in(key, 11)
    blocks = DEVICES
    key_full, key_perm, key_side = jax.random.split(key, 3)
    full_lane = jax.random.randint(key_full, (blocks, 1), 0, 3)
    perm_keys = jax.random.split(key_perm, blocks)
    placing = jax.vmap(permute_block)(perm_keys)
    side = jax.random.randint(key_side, (blocks, PAIRS_DEV), 0, 4)
    other = jnp.where(side < 3, 1, 2)
    lane = jnp.where(placing < CAP, full_lane, (full_lane + other) % 3)
    device = jnp.arange(blocks, dtype=jnp.int32) % DEVICES
    sector = device // N_SPAN
    owner = (sector[:, None] + lane - 1 + N_BLK) % N_BLK
    return owner.reshape(PAIRS, 1).astype(jnp.int32)


def set_ends(values, stream_key, low, top_value):
    dims = values.shape
    place = [jax.random.randint(jax.random.fold_in(stream_key, axis), (), 0, dims[axis]) for axis in range(len(dims))]
    values = values.at[tuple(place)].set(low)
    longest = dims.index(max(dims))
    place[longest] = (place[longest] + 1) % dims[longest]
    return values.at[tuple(place)].set(top_value)


def shard_levels(rng, extent, cuts, least, high):
    level = 1.0
    for axis_at, parts in cuts:
        steps = jax.random.uniform(jax.random.fold_in(jax.random.fold_in(rng, 6), axis_at), (parts,), jnp.float32, least / len(cuts), high / len(cuts))
        level = level * jnp.repeat(jnp.exp(steps), extent[axis_at] // parts).reshape((-1,) + (1,) * (len(extent) - 1 - axis_at))
    return level


def bell_draw(stream_key, shape, deviation, reach, pieces=(), kind=jnp.bfloat16):
    level = shard_levels(stream_key, shape, pieces, -0.22, 0.18) if pieces else 1.0
    values = jax.random.normal(stream_key, shape, jnp.float32) * deviation * level
    return jnp.minimum(jnp.maximum(values, -reach), reach).astype(kind)


def setup_inputs(seed: int = 0) -> dict:
    splits = jax.random.split(jax.random.key(seed), 8)
    fields = bell_draw(splits[0], (NV, NP, NP, NP, ELEMS), 1.0, 6.0, ((4, 512),), jnp.float32)
    jacobian = jnp.clip(jnp.exp(math.log(2.0) - 1.3862944 * jax.random.uniform(splits[1], (ELEMS,), jnp.float32) ** shard_levels(splits[1], (ELEMS,), ((0, 512),), -0.2, 0.2)), 0.5, 2.0)
    mean_flow = jnp.clip(jax.random.uniform(splits[2], (3,), jnp.float32, -0.5, 0.5), -0.5, 0.5)
    pair_owner = draw_pair_owner(jax.random.fold_in(splits[7], 71), 0)
    pair_mortar = set_ends(jax.random.randint(splits[4], (PAIRS,), 0, FS_DEV), jax.random.fold_in(splits[4], 1), 0, FS_DEV - 1).astype(jnp.int32)
    mortar_proj = bell_draw(splits[5], (2, 2, NP, NP), NP ** -0.5, 2.5, (), jnp.float32)
    coarse_id = set_ends(jax.random.randint(splits[6], (ELEMS,), 0, AGG_BLK), jax.random.fold_in(splits[6], 1), 0, AGG_BLK - 1).astype(jnp.int32)
    return dict(fields=fields, jacobian=jacobian, mean_flow=mean_flow, pair_owner=pair_owner, pair_mortar=pair_mortar, mortar_proj=mortar_proj, coarse_id=coarse_id)


time_step = 0.02
lift_scale = 15.0


def node_table():
    return np.array([-1.0, -0.7650553239294647, -0.2852315164806451, 0.2852315164806451, 0.7650553239294647, 1.0])


def weight_table():
    return np.array([1.0 / 15.0, 0.3784749562978470, 0.5548583770354863, 0.5548583770354863, 0.3784749562978470, 1.0 / 15.0])


def derivative_table():
    nodes = node_table()
    count = nodes.shape[0]
    barycentric = np.ones(count)
    for first in range(count):
        for other in range(count):
            if other != first:
                barycentric[first] = barycentric[first] / (nodes[first] - nodes[other])
    table = np.zeros((count, count))
    for row_index in range(count):
        for col_index in range(count):
            if row_index != col_index:
                table[row_index, col_index] = barycentric[col_index] / barycentric[row_index] / (nodes[row_index] - nodes[col_index])
        table[row_index, row_index] = -np.sum(table[row_index])
    return table


def coarse_table():
    return np.stack([weight_table(), weight_table() * node_table()])


def volume_term(fields, jacobian, mean_flow):
    deriv_table = jnp.asarray(derivative_table(), jnp.float32)
    grad_x = jnp.einsum("ai,vijke->vajke", deriv_table, fields, precision=lax.Precision.HIGHEST)
    grad_y = jnp.einsum("bj,vijke->vibke", deriv_table, fields, precision=lax.Precision.HIGHEST)
    grad_z = jnp.einsum("ck,vijke->vijce", deriv_table, fields, precision=lax.Precision.HIGHEST)
    advect = mean_flow[0] * grad_x + mean_flow[1] * grad_y + mean_flow[2] * grad_z
    spread = grad_x[1] + grad_y[2] + grad_z[3]
    result = jnp.stack([advect[0] + spread, advect[1] + grad_x[4], advect[2] + grad_y[4], advect[3] + grad_z[4], advect[4] + spread])
    return -jacobian * result


def normal_flux(trace, axial_flow):
    return jnp.stack([axial_flow * trace[0] + trace[3], axial_flow * trace[1], axial_flow * trace[2], axial_flow * trace[3] + trace[4], axial_flow * trace[4] + trace[3]])


def riemann(inner, outer, axial_flow):
    return 0.5 * (normal_flux(inner, axial_flow) + normal_flux(outer, axial_flow)) - 0.5 * (jnp.abs(axial_flow) + 1.0) * (outer - inner)


def project(side_mats, upper, trace):
    lower_part = jnp.einsum("ai,vijs->vajs", side_mats[0], trace, precision=lax.Precision.HIGHEST)
    upper_part = jnp.einsum("ai,vijs->vajs", side_mats[1], trace, precision=lax.Precision.HIGHEST)
    return jnp.where(upper, upper_part, lower_part)


def back_project(side_mats, upper, trace):
    lower_part = jnp.einsum("ia,vajs->vijs", side_mats[0], trace, precision=lax.Precision.HIGHEST)
    upper_part = jnp.einsum("ia,vajs->vijs", side_mats[1], trace, precision=lax.Precision.HIGHEST)
    return jnp.where(upper, upper_part, lower_part)


def coarse_modes(field, jacobian):
    weights = jnp.asarray(coarse_table(), jnp.float32)
    first = jnp.einsum("ai,vijke->vajke", weights, field, precision=lax.Precision.HIGHEST)
    second = jnp.einsum("bj,vajke->vabke", weights, first, precision=lax.Precision.HIGHEST)
    third = jnp.einsum("ck,vabke->vabce", weights, second, precision=lax.Precision.HIGHEST)
    scaled = third / (jacobian * jacobian * jacobian)
    return scaled.reshape(NV * 8, field.shape[4])


def global_residual(fields, jacobian, mean_flow, owner_all, mortar_all, matrices):
    face_count = E_DEV // 4
    axial_flow = mean_flow[2]

    def volume_block(index, total):
        start = (index * E_DEV).astype(jnp.int32)
        block = lax.dynamic_slice_in_dim(fields, start, E_DEV, 4)
        scale = lax.dynamic_slice_in_dim(jacobian, start, E_DEV, 0)
        return lax.dynamic_update_slice_in_dim(total, volume_term(block, scale, mean_flow), start, 4)

    volume = lax.fori_loop(0, DEVICES, volume_block, jnp.zeros_like(fields))
    shaped = fields.reshape(NV, NP, NP, NP, DEVICES, E_DEV)
    rotor_trace = shaped[:, :, :, 5, :, :face_count]
    stator_trace = shaped[:, :, :, 0, :, face_count:2 * face_count]
    pair_trace = jnp.repeat(rotor_trace, 2, axis=4).reshape(NV, NP, NP, PAIRS)
    device_of_pair = jnp.arange(PAIRS, dtype=jnp.int32) // PAIRS_DEV
    stator_index = (owner_all * N_SPAN + device_of_pair % N_SPAN) * face_count + mortar_all
    stator_flat = stator_trace.reshape(NV, NP, NP, DEVICES * face_count)
    stator_pair = jnp.take(stator_flat, stator_index, axis=3)
    upper = jnp.arange(PAIRS, dtype=jnp.int32) % 2 == 1
    mortar_flux = riemann(project(matrices[0], upper, pair_trace), project(matrices[1], upper, stator_pair), axial_flow)
    rotor_sum = back_project(matrices[0], upper, mortar_flux).reshape(NV, NP, NP, DEVICES, face_count, 2).sum(axis=5)
    stator_terms = jnp.moveaxis(back_project(matrices[1], upper, mortar_flux), 3, 0)
    stator_sum = jax.ops.segment_sum(stator_terms, stator_index, num_segments=DEVICES * face_count)
    stator_sum = jnp.moveaxis(stator_sum, 0, 3).reshape(NV, NP, NP, DEVICES, face_count)
    jac_shaped = jacobian.reshape(DEVICES, E_DEV)
    rotor_lift = lift_scale * jac_shaped[:, :face_count] * (normal_flux(rotor_trace, axial_flow) - rotor_sum)
    stator_lift = lift_scale * jac_shaped[:, face_count:2 * face_count] * (stator_sum - normal_flux(stator_trace, axial_flow))
    volume = volume.reshape(NV, NP, NP, NP, DEVICES, E_DEV)
    volume = volume.at[:, :, :, 5, :, :face_count].add(rotor_lift)
    volume = volume.at[:, :, :, 0, :, face_count:2 * face_count].add(stator_lift)
    return volume.reshape(fields.shape)


def reference(fields, jacobian, mean_flow, pair_owner, pair_mortar, mortar_proj, coarse_id):
    owner_all = pair_owner[:, 0]
    first_rate = global_residual(fields, jacobian, mean_flow, owner_all, pair_mortar, mortar_proj)
    section_one = fields + time_step * first_rate
    second_rate = global_residual(section_one, jacobian, mean_flow, owner_all, pair_mortar, mortar_proj)
    new_fields = 0.5 * fields + 0.5 * (section_one + time_step * second_rate)
    combined = 0.5 * first_rate + 0.5 * second_rate
    modes = coarse_modes(combined, jacobian)
    sector = jnp.arange(ELEMS, dtype=jnp.int32) // (E_DEV * N_SPAN)
    target = sector * AGG_BLK + coarse_id
    coarse_residual = jax.ops.segment_sum(modes.T, target, num_segments=AGGS).T
    return new_fields, coarse_residual
```

```python
import jax
import jax.numpy as jnp
import numpy as np
from jax import lax
from jax.experimental import pallas as pl
from jax.experimental.pallas import tpu as pltpu
from jax.sharding import PartitionSpec as P

NP = 6
NV = 5
FACES = 64
LANES = 128
ROWS = NV * NP * NP
CODES, FIRST, SECOND, ONES = ROWS, ROWS + 1, ROWS + 2, ROWS + 3
MSG = ROWS + 4

time_step = 0.02
lift_scale = 15.0

PARTNERS = ({0: 1, 1: 4, 4: 1}, {0: 2, 2: 4, 4: 2}, {0: 3, 3: 4, 4: 3})


def node_table():
    return np.array(
        [
            -1.0,
            -0.7650553239294647,
            -0.2852315164806451,
            0.2852315164806451,
            0.7650553239294647,
            1.0,
        ]
    )


def weight_table():
    return np.array(
        [
            1.0 / 15.0,
            0.378474956297847,
            0.5548583770354863,
            0.5548583770354863,
            0.378474956297847,
            1.0 / 15.0,
        ]
    )


def derivative_table():
    nodes = node_table()
    count = nodes.shape[0]
    barycentric = np.ones(count)
    for first in range(count):
        for other in range(count):
            if other != first:
                barycentric[first] = barycentric[first] / (nodes[first] - nodes[other])
    table = np.zeros((count, count))
    for row_index in range(count):
        for col_index in range(count):
            if row_index != col_index:
                table[row_index, col_index] = (
                    barycentric[col_index]
                    / barycentric[row_index]
                    / (nodes[row_index] - nodes[col_index])
                )
        table[row_index, row_index] = -np.sum(table[row_index])
    return table


DERIV = derivative_table()
ODD = [[0.5 * float(DERIV[a, m] - DERIV[a, 5 - m]) for m in range(3)] for a in range(3)]
EVEN = [[0.5 * float(DERIV[a, m] + DERIV[a, 5 - m]) for m in range(3)] for a in range(3)]
COARSE = [[float(w) for w in row] for row in (weight_table(), weight_table() * node_table())]


def derivative(tiles):
    even = [tiles[m] + tiles[5 - m] for m in range(3)]
    odd = [tiles[m] - tiles[5 - m] for m in range(3)]
    result = [None] * 6
    for a in range(3):
        s = ODD[a][0] * odd[0] + ODD[a][1] * odd[1] + ODD[a][2] * odd[2]
        d = EVEN[a][0] * even[0] + EVEN[a][1] * even[1] + EVEN[a][2] * even[2]
        result[a] = s + d
        result[5 - a] = s - d
    return result


def moments(tiles):
    even = [tiles[m] + tiles[5 - m] for m in range(3)]
    odd = [tiles[m] - tiles[5 - m] for m in range(3)]
    return [
        COARSE[0][0] * even[0] + COARSE[0][1] * even[1] + COARSE[0][2] * even[2],
        COARSE[1][0] * odd[0] + COARSE[1][1] * odd[1] + COARSE[1][2] * odd[2],
    ]


def flux_tiles(direction, v, speed, load):
    tiles = load(v)
    partner = PARTNERS[direction].get(v)
    if partner is None:
        return [speed * t for t in tiles]
    return [speed * t + o for t, o in zip(tiles, load(partner))]


def column(values):
    at = lax.broadcasted_iota(jnp.int32, (6, 1), 0)
    result = jnp.full((6, 1), values[0], jnp.float32)
    for k in range(1, 6):
        result = jnp.where(at == k, values[k], result)
    return result


def tile(v, i, j):
    return ((v * NP + i) * NP + j) * 8


def volume_passes(flow_ref, q, acc, finish):
    u = [flow_ref[d] for d in range(3)]

    for i in range(NP):
        def load(v, i=i):
            return [q[pl.ds(tile(v, i, 0) + k, 6, stride=8), :] for k in range(6)]

        for v in range(NV):
            out = derivative(flux_tiles(2, v, u[2], load))
            for k in range(6):
                acc[pl.ds(tile(v, i, 0) + k, 6, stride=8), :] = out[k]

    for j in range(NP):
        def load(v, j=j):
            return [q[pl.ds(tile(v, i, j), 8), :] for i in range(6)]

        for v in range(NV):
            out = derivative(flux_tiles(0, v, u[0], load))
            for i in range(6):
                acc[pl.ds(tile(v, i, j), 8), :] += out[i]

    for v in range(NV):
        for i in range(NP):
            def load(w, i=i):
                return [q[pl.ds(tile(w, i, j), 8), :] for j in range(6)]

            out = derivative(flux_tiles(1, v, u[1], load))
            finish(v, i, [acc[pl.ds(tile(v, i, j), 8), :] + out[j] for j in range(6)])


def message_kernel(here_ref, fields_ref, owner_ref, mortar_ref, message_ref):
    lane = lax.broadcasted_iota(jnp.int32, (NP, LANES), 1)
    rotor = lane < FACES
    for v in range(NV):
        for i in range(NP):
            block = fields_ref[v, i]
            message_ref[pl.ds((v * NP + i) * NP, 6), :] = jnp.where(
                rotor, block[:, 5, :], block[:, 0, :]
            )
    sectors = here_ref[1]
    step = owner_ref[...] - here_ref[0]
    after = (step == 1) | (step == 1 - sectors)
    side = jnp.where(step == 0, 1, jnp.where(after, 2, 0))
    code = (side * FACES + mortar_ref[...]).astype(jnp.float32)
    source = lax.broadcasted_iota(jnp.int32, (LANES, 3 * LANES), 0)
    target = lax.broadcasted_iota(jnp.int32, (LANES, 3 * LANES), 1)
    face = target % FACES
    half = jnp.where(target < LANES, (target // FACES) % 2, target // LANES - 1)
    select = (source == 2 * face + half).astype(jnp.float32).astype(jnp.bfloat16)
    code = jnp.broadcast_to(code, (8, LANES)).astype(jnp.bfloat16)
    rows = jnp.dot(code, select, preferred_element_type=jnp.float32)
    message_ref[CODES : CODES + 1, :] = rows[0:1, 0:LANES]
    message_ref[FIRST : FIRST + 1, :] = rows[0:1, LANES : 2 * LANES]
    message_ref[SECOND : SECOND + 1, :] = rows[0:1, 2 * LANES : 3 * LANES]
    message_ref[ONES : ONES + 1, :] = jnp.ones((1, LANES), jnp.float32)


def coefficient_rows(mats_ref, table_ref):
    lane = lax.broadcasted_iota(jnp.int32, (1, LANES), 1)
    rotor = lane < FACES

    def entry(side, h, a, i):
        return mats_ref[((side * 2 + h) * NP + a) * NP + i]

    for h in range(2):
        own = [
            [jnp.where(rotor, entry(0, h, a, i), entry(1, h, a, i)) for i in range(6)]
            for a in range(6)
        ]
        other = [
            [jnp.where(rotor, entry(1, h, a, i), entry(0, h, a, i)) for i in range(6)]
            for a in range(6)
        ]
        for i in range(6):
            for m in range(6):
                cross = own[i][0] * other[0][m]
                square = own[i][0] * own[0][m]
                for a in range(1, 6):
                    cross = cross + own[i][a] * other[a][m]
                    square = square + own[i][a] * own[a][m]
                row = h * 36 + i * 6 + m
                table_ref[row : row + 1, :] = cross
                table_ref[72 + row : 73 + row, :] = square


def first_volume_kernel(
    flow_ref, mats_ref, fields_ref, jac_ref, rate_ref, trace_ref, table_ref, q, acc
):
    for v in range(NV):
        for i in range(NP):
            for j in range(NP):
                q[pl.ds(tile(v, i, j), 6), :] = fields_ref[v, i, j]
    scale = -time_step * jac_ref[...]

    def finish(v, i, tiles):
        for j in range(6):
            value = scale * tiles[j]
            rate_ref[v, i, j] = value[0:6]
            acc[pl.ds(tile(v, i, j), 8), :] = value

    volume_passes(flow_ref, q, acc, finish)

    @pl.when(pl.program_id(0) == 0)
    def _():
        lane = lax.broadcasted_iota(jnp.int32, (NP, LANES), 1)
        rotor = lane < FACES
        for v in range(NV):
            for i in range(NP):
                at = tile(v, i, 0)
                top = pl.ds(at + 5, 6, stride=8)
                bottom = pl.ds(at, 6, stride=8)
                trace_ref[pl.ds((v * NP + i) * NP, 6), :] = jnp.where(
                    rotor, q[top, :] + acc[top, :], q[bottom, :] + acc[bottom, :]
                )
        coefficient_rows(mats_ref, table_ref)


def layer_mask():
    node = lax.broadcasted_iota(jnp.int32, (NP, LANES), 0)
    lane = lax.broadcasted_iota(jnp.int32, (NP, LANES), 1)
    hit = ((node == 5) & (lane < FACES)) | ((node == 0) & (lane >= FACES))
    return jnp.where(hit, 1.0, 0.0)


def second_volume_kernel(
    flow_ref, fields_ref, jac_ref, rate_ref, lift_ref, new_ref, modes_ref, q, acc
):
    mask = layer_mask() * jnp.where(pl.program_id(0) == 0, 1.0, 0.0)
    for v in range(NV):
        for i in range(NP):
            for j in range(NP):
                row = (v * NP + i) * NP + j
                layer = jnp.broadcast_to(lift_ref[row : row + 1, :], (NP, LANES))
                q[pl.ds(tile(v, i, j), 6), :] = (
                    fields_ref[v, i, j] + rate_ref[v, i, j] + mask * layer
                )
    jac = jac_ref[...]
    scale = -time_step * jac
    weight = (0.5 / time_step) / (jac * jac * jac)
    columns = [column(COARSE[c]) for c in range(2)]
    sums = {}

    def finish(v, i, tiles):
        change = []
        for j in range(6):
            base = fields_ref[v, i, j]
            first = q[pl.ds(tile(v, i, j), 6), :] - base
            both = first + scale * tiles[j][0:6]
            new_ref[v, i, j] = base + 0.5 * both
            change.append(both)
        for b, value in enumerate(moments(change)):
            for a in range(2):
                term = COARSE[a][i] * value
                sums[a, b] = term if i == 0 else sums[a, b] + term
        if i == 5:
            for a in range(2):
                for b in range(2):
                    for c in range(2):
                        row = v * 8 + a * 4 + b * 2 + c
                        total = jnp.sum(columns[c] * sums[a, b], axis=0, keepdims=True)
                        modes_ref[row : row + 1, :] = weight * total

    volume_passes(flow_ref, q, acc, finish)


def split(value):
    high = value.astype(jnp.bfloat16)
    low = (value - high.astype(jnp.float32)).astype(jnp.bfloat16)
    return high, low


def pair_matrix(left_ref, own_ref, right_ref, pick):
    lane = lax.broadcasted_iota(jnp.int32, (FACES, LANES), 1)
    face = lax.broadcasted_iota(jnp.int32, (FACES, LANES), 0).astype(jnp.float32)
    stator = lane >= FACES
    own = [own_ref[row : row + 1, :] for row in (FIRST, SECOND)]
    for device, ref in enumerate((left_ref, own_ref, right_ref)):
        code = jnp.broadcast_to(ref[CODES : CODES + 1, :], (LANES, LANES)).T
        offset = (2 - device) * FACES
        target = jnp.where(stator, lane - FACES + offset, -1).astype(jnp.float32)
        for h in range(2):
            top = jnp.where(code[h * FACES : (h + 1) * FACES] == target, 1.0, 0.0)
            mine = jnp.where(stator, -1.0, jnp.broadcast_to(own[h], (FACES, LANES)))
            bottom = jnp.where(mine == face + float(device * FACES), 1.0, 0.0)
            columns = slice(h * LANES, (h + 1) * LANES)
            at = device * LANES
            pick[at : at + FACES, columns] = top.astype(jnp.bfloat16)
            pick[at + FACES : at + LANES, columns] = bottom.astype(jnp.bfloat16)


def lift_rows(flow_ref, left_ref, own_ref, right_ref, pick, table_ref, jac_ref, work, coef, emit):
    high, low = split(
        jnp.concatenate([left_ref[...], own_ref[...], right_ref[...]], axis=1)
    )
    matrix = pick[...]
    work[...] = jnp.dot(high, matrix, preferred_element_type=jnp.float32) + jnp.dot(
        low, matrix, preferred_element_type=jnp.float32
    )
    coef[...] = (
        work[ONES : ONES + 1, 0:LANES] * table_ref[72:108, :]
        + work[ONES : ONES + 1, LANES : 2 * LANES] * table_ref[108:144, :]
    )
    axial = flow_ref[2]
    speed = 0.5 * (jnp.abs(axial) + 1.0)
    lane = lax.broadcasted_iota(jnp.int32, (1, LANES), 1)
    scale = (time_step * lift_scale) * jac_ref[:, 0:LANES]
    signed = jnp.where(lane < FACES, scale, -scale)
    damp = speed * scale
    for i in range(NP):
        cross = [
            [table_ref[h * 36 + i * 6 + m : h * 36 + i * 6 + m + 1, :] for m in range(6)]
            for h in range(2)
        ]
        square = [coef[i * 6 + m : i * 6 + m + 1, :] for m in range(6)]
        mean, jump = [], []
        for v in range(NV):
            other = None
            own = None
            for m in range(6):
                rows = pl.ds((v * NP + m) * NP, 6)
                term = cross[0][m] * work[rows, 0:LANES]
                term = term + cross[1][m] * work[rows, LANES : 2 * LANES]
                other = term if other is None else other + term
                term = square[m] * own_ref[rows, :]
                own = term if own is None else own + term
            mean.append(own_ref[pl.ds((v * NP + i) * NP, 6), :] - 0.5 * (own + other))
            jump.append(own - other)
        for v in range(NV):
            flux = axial * mean[v]
            partner = PARTNERS[2].get(v)
            if partner is not None:
                flux = flux + mean[partner]
            emit(v, i, signed * flux - damp * jump[v])


def first_lift_kernel(
    flow_ref, left_ref, own_ref, right_ref, trace_ref, table_ref, jac_ref,
    message_ref, lift_ref, pick, work, coef,
):
    pair_matrix(left_ref, own_ref, right_ref, pick)

    def emit(v, i, value):
        rows = pl.ds((v * NP + i) * NP, 6)
        lift_ref[rows, :] = value
        message_ref[rows, :] = trace_ref[rows, :] + value

    lift_rows(
        flow_ref, left_ref, own_ref, right_ref, pick, table_ref, jac_ref, work, coef, emit
    )
    message_ref[ROWS:MSG, :] = own_ref[ROWS:MSG, :]


def second_lift_kernel(
    flow_ref, left_ref, own_ref, right_ref, pick, table_ref, jac_ref, modes_ref, agg_ref, base_ref,
    new_ref, sums_ref, work, coef,
):
    mask = 0.5 * layer_mask()
    sums = {}

    def emit(v, i, value):
        for j in range(6):
            new_ref[v, i, j] = base_ref[v, i, j] + mask * jnp.broadcast_to(
                value[j : j + 1, :], (NP, LANES)
            )
        for a in range(2):
            term = COARSE[a][i] * value
            sums[v, a] = term if i == 0 else sums[v, a] + term

    lift_rows(
        flow_ref, left_ref, own_ref, right_ref, pick, table_ref, jac_ref, work, coef, emit
    )
    lane = lax.broadcasted_iota(jnp.int32, (1, LANES), 1)
    jac = jac_ref[:, 0:LANES]
    weight = (0.5 / time_step) / (jac * jac * jac)
    ends = [weight * jnp.where(lane < FACES, COARSE[c][5], COARSE[c][0]) for c in range(2)]
    columns = [column(COARSE[b]) for b in range(2)]
    rows = []
    for v in range(NV):
        for a in range(2):
            for b in range(2):
                total = jnp.sum(columns[b] * sums[v, a], axis=0, keepdims=True)
                for c in range(2):
                    rows.append(ends[c] * total)
    count = 8 * NV
    at = lax.broadcasted_iota(jnp.int32, (8, LANES), 0)
    blocks = []
    for v in range(NV):
        block = jnp.broadcast_to(rows[v * 8], (8, LANES))
        for r in range(1, 8):
            block = jnp.where(at == r, rows[v * 8 + r], block)
        blocks.append(block)
    faces = modes_ref[:, 0:LANES] + jnp.concatenate(blocks, axis=0)
    modes = jnp.concatenate([faces, modes_ref[:, LANES:]], axis=1)
    high, low = split(modes)
    aggs = sums_ref.shape[0] * sums_ref.shape[1]
    name = lax.broadcasted_iota(jnp.int32, (aggs, modes.shape[1]), 0)
    member = jnp.where(name == agg_ref[...], 1.0, 0.0).astype(jnp.bfloat16)
    contract = (((1,), (1,)), ((), ()))
    total = lax.dot_general(
        member, high, contract, preferred_element_type=jnp.float32
    ) + lax.dot_general(member, low, contract, preferred_element_type=jnp.float32)
    share = sums_ref.shape[1]
    for s in range(sums_ref.shape[0]):
        sums_ref[s] = total[s * share : (s + 1) * share, :]


def shifted(value, axis, steps):
    count = lax.axis_size(axis)
    pairs = [(source, (source + steps) % count) for source in range(count)]
    return lax.ppermute(value, axis, pairs)


VMEM = pl.BlockSpec(memory_space=pltpu.VMEM)
SMEM = pl.BlockSpec(memory_space=pltpu.SMEM)


def shape(*dims, dtype=jnp.float32):
    return jax.ShapeDtypeStruct(dims, dtype)


def params():
    return pltpu.CompilerParams(vmem_limit_bytes=48 * 1024 * 1024)


def local(fields, jacobian, mean_flow, pair_owner, pair_mortar, mortar_proj, coarse_id):
    elements = fields.shape[4]
    spans = lax.axis_size("span")
    aggs = elements * spans // 8
    jac_row = jacobian.reshape(1, elements)
    mats = mortar_proj.reshape(4 * NP * NP)
    here = jnp.stack([lax.axis_index("blk"), lax.axis_size("blk")]).astype(jnp.int32)
    dims = (NV, NP, NP, NP, LANES)
    half = pl.BlockSpec(dims, lambda n: (0, 0, 0, 0, n))
    row = pl.BlockSpec((1, LANES), lambda n: (0, n))
    whole = pl.BlockSpec((MSG, LANES), lambda n: (0, 0))
    face_half = pl.BlockSpec(dims, lambda n: (0, 0, 0, 0, 0))
    fixed = lambda *d: pl.BlockSpec(d, lambda n: (0,) * len(d))
    tiles = pltpu.VMEM((NV * NP * NP * 8, LANES), jnp.float32)
    grid = (elements // LANES,)
    volume_cost = pl.CostEstimate(
        flops=120 * NV * 216 * elements, bytes_accessed=3 * 4 * 1440 * elements, transcendentals=0
    )

    message = pl.pallas_call(
        message_kernel,
        grid=(1,),
        in_specs=[SMEM, face_half, fixed(1, LANES), fixed(1, LANES)],
        out_specs=whole,
        out_shape=shape(MSG, LANES),
        compiler_params=params(),
        name="face_message",
    )(here, fields, pair_owner.reshape(1, LANES), pair_mortar.reshape(1, LANES))
    left = shifted(message, "blk", 1)
    right = shifted(message, "blk", -1)

    rate, trace, table = pl.pallas_call(
        first_volume_kernel,
        grid=grid,
        in_specs=[SMEM, SMEM, half, row],
        out_specs=[half, whole, fixed(144, LANES)],
        out_shape=[shape(*fields.shape), shape(MSG, LANES), shape(144, LANES)],
        scratch_shapes=[tiles, tiles],
        compiler_params=params(),
        cost_estimate=volume_cost,
        name="first_volume",
    )(mean_flow, mats, fields, jac_row)

    message2, lift, pick = pl.pallas_call(
        first_lift_kernel,
        in_specs=[SMEM] + [VMEM] * 6,
        out_specs=[VMEM] * 3,
        out_shape=[
            shape(MSG, LANES),
            shape(ROWS, LANES),
            shape(3 * LANES, 2 * LANES, dtype=jnp.bfloat16),
        ],
        scratch_shapes=[
            pltpu.VMEM((MSG, 2 * LANES), jnp.float32),
            pltpu.VMEM((36, LANES), jnp.float32),
        ],
        compiler_params=params(),
        name="first_lift",
    )(mean_flow, left, message, right, trace, table, jac_row)
    left2 = shifted(message2, "blk", 1)
    right2 = shifted(message2, "blk", -1)

    base, modes = pl.pallas_call(
        second_volume_kernel,
        grid=grid,
        in_specs=[SMEM, half, row, half, fixed(ROWS, LANES)],
        out_specs=[half, pl.BlockSpec((8 * NV, LANES), lambda n: (0, n))],
        out_shape=[shape(*fields.shape), shape(8 * NV, elements)],
        scratch_shapes=[tiles, tiles],
        compiler_params=params(),
        cost_estimate=volume_cost,
        name="second_volume",
    )(mean_flow, fields, jac_row, rate, lift)

    new_fields, sums = pl.pallas_call(
        second_lift_kernel,
        grid=(1,),
        in_specs=[
            SMEM,
            whole,
            whole,
            whole,
            fixed(3 * LANES, 2 * LANES),
            fixed(144, LANES),
            fixed(1, elements),
            fixed(8 * NV, elements),
            fixed(1, elements),
            face_half,
        ],
        out_specs=[face_half, fixed(spans, aggs // spans, 8 * NV)],
        out_shape=[shape(*fields.shape), shape(spans, aggs // spans, 8 * NV)],
        scratch_shapes=[
            pltpu.VMEM((MSG, 2 * LANES), jnp.float32),
            pltpu.VMEM((36, LANES), jnp.float32),
        ],
        input_output_aliases={9: 0},
        compiler_params=params(),
        name="second_lift",
    )(
        mean_flow, left2, message2, right2, pick, table, jac_row, modes,
        coarse_id.reshape(1, elements), base,
    )
    parts = lax.all_to_all(sums, "span", 0, 0)
    return new_fields, jnp.sum(parts, axis=0).T


def solution(mesh):
    return jax.shard_map(
        local,
        mesh=mesh,
        in_specs=(
            P(None, None, None, None, ("blk", "span")),
            P(("blk", "span")),
            P(),
            P(("blk", "span"), None),
            P(("blk", "span")),
            P(),
            P(("blk", "span")),
        ),
        out_specs=(P(None, None, None, None, ("blk", "span")), P(None, ("blk", "span"))),
        check_vma=False,
    )
```

```python
import jax
import jax.numpy as jnp
import numpy as np
from jax import lax
from jax.experimental import pallas as pl
from jax.experimental.pallas import tpu as pltpu
from jax.sharding import PartitionSpec as P

NP = 6
NV = 5
FACES = 64
LANES = 128
ROWS = NV * NP * NP
CODES, FIRST, SECOND, ONES = ROWS, ROWS + 1, ROWS + 2, ROWS + 3
MSG = ROWS + 4

time_step = 0.02
lift_scale = 15.0

PARTNERS = ({0: 1, 1: 4, 4: 1}, {0: 2, 2: 4, 4: 2}, {0: 3, 3: 4, 4: 3})


def node_table():
    return np.array(
        [
            -1.0,
            -0.7650553239294647,
            -0.2852315164806451,
            0.2852315164806451,
            0.7650553239294647,
            1.0,
        ]
    )


def weight_table():
    return np.array(
        [
            1.0 / 15.0,
            0.378474956297847,
            0.5548583770354863,
            0.5548583770354863,
            0.378474956297847,
            1.0 / 15.0,
        ]
    )


def derivative_table():
    nodes = node_table()
    count = nodes.shape[0]
    barycentric = np.ones(count)
    for first in range(count):
        for other in range(count):
            if other != first:
                barycentric[first] = barycentric[first] / (nodes[first] - nodes[other])
    table = np.zeros((count, count))
    for row_index in range(count):
        for col_index in range(count):
            if row_index != col_index:
                table[row_index, col_index] = (
                    barycentric[col_index]
                    / barycentric[row_index]
                    / (nodes[row_index] - nodes[col_index])
                )
        table[row_index, row_index] = -np.sum(table[row_index])
    return table


DERIV = derivative_table()
ODD = [[0.5 * float(DERIV[a, m] - DERIV[a, 5 - m]) for m in range(3)] for a in range(3)]
EVEN = [[0.5 * float(DERIV[a, m] + DERIV[a, 5 - m]) for m in range(3)] for a in range(3)]
COARSE = [[float(w) for w in row] for row in (weight_table(), weight_table() * node_table())]


def derivative(tiles):
    even = [tiles[m] + tiles[5 - m] for m in range(3)]
    odd = [tiles[m] - tiles[5 - m] for m in range(3)]
    result = [None] * 6
    for a in range(3):
        s = ODD[a][0] * odd[0] + ODD[a][1] * odd[1] + ODD[a][2] * odd[2]
        d = EVEN[a][0] * even[0] + EVEN[a][1] * even[1] + EVEN[a][2] * even[2]
        result[a] = s + d
        result[5 - a] = s - d
    return result


def moments(tiles):
    even = [tiles[m] + tiles[5 - m] for m in range(3)]
    odd = [tiles[m] - tiles[5 - m] for m in range(3)]
    return [
        COARSE[0][0] * even[0] + COARSE[0][1] * even[1] + COARSE[0][2] * even[2],
        COARSE[1][0] * odd[0] + COARSE[1][1] * odd[1] + COARSE[1][2] * odd[2],
    ]


def flux_tiles(direction, v, speed, load):
    tiles = load(v)
    partner = PARTNERS[direction].get(v)
    if partner is None:
        return [speed * t for t in tiles]
    return [speed * t + o for t, o in zip(tiles, load(partner))]


def column(values):
    at = lax.broadcasted_iota(jnp.int32, (6, 1), 0)
    result = jnp.full((6, 1), values[0], jnp.float32)
    for k in range(1, 6):
        result = jnp.where(at == k, values[k], result)
    return result


def tile(v, i, j):
    return ((v * NP + i) * NP + j) * 8


def volume_passes(flow_ref, q, acc, finish):
    u = [flow_ref[d] for d in range(3)]

    for i in range(NP):
        def load(v, i=i):
            return [q[pl.ds(tile(v, i, 0) + k, 6, stride=8), :] for k in range(6)]

        for v in range(NV):
            out = derivative(flux_tiles(2, v, u[2], load))
            for k in range(6):
                acc[pl.ds(tile(v, i, 0) + k, 6, stride=8), :] = out[k]

    for j in range(NP):
        def load(v, j=j):
            return [q[pl.ds(tile(v, i, j), 8), :] for i in range(6)]

        for v in range(NV):
            out = derivative(flux_tiles(0, v, u[0], load))
            for i in range(6):
                acc[pl.ds(tile(v, i, j), 8), :] += out[i]

    for v in range(NV):
        for i in range(NP):
            def load(w, i=i):
                return [q[pl.ds(tile(w, i, j), 8), :] for j in range(6)]

            out = derivative(flux_tiles(1, v, u[1], load))
            finish(v, i, [acc[pl.ds(tile(v, i, j), 8), :] + out[j] for j in range(6)])


def message_kernel(
    fields_hbm, owner_hbm, mortar_hbm, message_ref, fields_ref, owner_ref, mortar_ref, sems
):
    copies = [
        pltpu.make_async_copy(owner_hbm, owner_ref, sems.at[0]),
        pltpu.make_async_copy(mortar_hbm, mortar_ref, sems.at[1]),
        pltpu.make_async_copy(fields_hbm.at[:, :, :, :, pl.ds(0, LANES)], fields_ref, sems.at[2]),
    ]
    for copy in copies:
        copy.start()
    copies[0].wait()
    copies[1].wait()
    pair_codes(owner_ref, mortar_ref, message_ref)
    copies[2].wait()
    lane = lax.broadcasted_iota(jnp.int32, (NP, LANES), 1)
    rotor = lane < FACES
    for v in range(NV):
        for i in range(NP):
            block = fields_ref[v, i]
            message_ref[pl.ds((v * NP + i) * NP, 6), :] = jnp.where(
                rotor, block[:, 5, :], block[:, 0, :]
            )


def pair_codes(owner_ref, mortar_ref, message_ref):
    sectors = lax.axis_size("blk")
    step = owner_ref[...] - lax.axis_index("blk")
    after = (step == 1) | (step == 1 - sectors)
    side = jnp.where(step == 0, 1, jnp.where(after, 2, 0))
    code = (side * FACES + mortar_ref[...]).astype(jnp.float32)
    source = lax.broadcasted_iota(jnp.int32, (LANES, 3 * LANES), 0)
    target = lax.broadcasted_iota(jnp.int32, (LANES, 3 * LANES), 1)
    face = target % FACES
    half = jnp.where(target < LANES, (target // FACES) % 2, target // LANES - 1)
    select = (source == 2 * face + half).astype(jnp.float32).astype(jnp.bfloat16)
    code = jnp.broadcast_to(code, (8, LANES)).astype(jnp.bfloat16)
    rows = jnp.dot(code, select, preferred_element_type=jnp.float32)
    message_ref[CODES : CODES + 1, :] = rows[0:1, 0:LANES]
    message_ref[FIRST : FIRST + 1, :] = rows[0:1, LANES : 2 * LANES]
    message_ref[SECOND : SECOND + 1, :] = rows[0:1, 2 * LANES : 3 * LANES]
    message_ref[ONES : ONES + 1, :] = jnp.ones((1, LANES), jnp.float32)


def coefficient_rows(mats_ref, table_ref):
    lane = lax.broadcasted_iota(jnp.int32, (1, LANES), 1)
    rotor = lane < FACES

    def entry(side, h, a, i):
        return mats_ref[((side * 2 + h) * NP + a) * NP + i]

    for h in range(2):
        own = [
            [jnp.where(rotor, entry(0, h, a, i), entry(1, h, a, i)) for i in range(6)]
            for a in range(6)
        ]
        other = [
            [jnp.where(rotor, entry(1, h, a, i), entry(0, h, a, i)) for i in range(6)]
            for a in range(6)
        ]
        for i in range(6):
            for m in range(6):
                cross = own[i][0] * other[0][m]
                square = own[i][0] * own[0][m]
                for a in range(1, 6):
                    cross = cross + own[i][a] * other[a][m]
                    square = square + own[i][a] * own[a][m]
                row = h * 36 + i * 6 + m
                table_ref[row : row + 1, :] = cross
                table_ref[72 + row : 73 + row, :] = square


def first_volume_kernel(
    flow_ref, mats_ref, fields_ref, jac_ref, rate_ref, trace_ref, table_ref, q, acc
):
    for v in range(NV):
        for i in range(NP):
            for j in range(NP):
                q[pl.ds(tile(v, i, j), 6), :] = fields_ref[v, i, j]
    scale = -time_step * jac_ref[...]

    def finish(v, i, tiles):
        for j in range(6):
            value = scale * tiles[j]
            rate_ref[v, i, j] = value[0:6]
            acc[pl.ds(tile(v, i, j), 8), :] = value

    volume_passes(flow_ref, q, acc, finish)

    @pl.when(pl.program_id(0) == 0)
    def _():
        lane = lax.broadcasted_iota(jnp.int32, (NP, LANES), 1)
        rotor = lane < FACES
        for v in range(NV):
            for i in range(NP):
                at = tile(v, i, 0)
                top = pl.ds(at + 5, 6, stride=8)
                bottom = pl.ds(at, 6, stride=8)
                trace_ref[pl.ds((v * NP + i) * NP, 6), :] = jnp.where(
                    rotor, q[top, :] + acc[top, :], q[bottom, :] + acc[bottom, :]
                )
        coefficient_rows(mats_ref, table_ref)


def layer_mask():
    node = lax.broadcasted_iota(jnp.int32, (NP, LANES), 0)
    lane = lax.broadcasted_iota(jnp.int32, (NP, LANES), 1)
    hit = ((node == 5) & (lane < FACES)) | ((node == 0) & (lane >= FACES))
    return jnp.where(hit, 1.0, 0.0)


def second_volume_kernel(
    flow_ref, fields_ref, jac_ref, rate_ref, lift_ref, new_ref, modes_ref, q, acc
):
    mask = layer_mask() * jnp.where(pl.program_id(0) == 0, 1.0, 0.0)
    for v in range(NV):
        for i in range(NP):
            for j in range(NP):
                row = (v * NP + i) * NP + j
                layer = jnp.broadcast_to(lift_ref[row : row + 1, :], (NP, LANES))
                q[pl.ds(tile(v, i, j), 6), :] = (
                    fields_ref[v, i, j] + rate_ref[v, i, j] + mask * layer
                )
    jac = jac_ref[...]
    scale = -time_step * jac
    weight = (0.5 / time_step) / (jac * jac * jac)
    columns = [column(COARSE[c]) for c in range(2)]
    sums = {}

    def finish(v, i, tiles):
        change = []
        for j in range(6):
            base = fields_ref[v, i, j]
            first = q[pl.ds(tile(v, i, j), 6), :] - base
            both = first + scale * tiles[j][0:6]
            new_ref[v, i, j] = base + 0.5 * both
            change.append(both)
        for b, value in enumerate(moments(change)):
            for a in range(2):
                term = COARSE[a][i] * value
                sums[a, b] = term if i == 0 else sums[a, b] + term
        if i == 5:
            for a in range(2):
                for b in range(2):
                    for c in range(2):
                        row = v * 8 + a * 4 + b * 2 + c
                        total = jnp.sum(columns[c] * sums[a, b], axis=0, keepdims=True)
                        modes_ref[row : row + 1, :] = weight * total

    volume_passes(flow_ref, q, acc, finish)


def split(value):
    high = value.astype(jnp.bfloat16)
    low = (value - high.astype(jnp.float32)).astype(jnp.bfloat16)
    return high, low


def pair_matrix(first_ref, own_ref, second_ref, pick):
    lane = lax.broadcasted_iota(jnp.int32, (FACES, LANES), 1)
    face = lax.broadcasted_iota(jnp.int32, (FACES, LANES), 0).astype(jnp.float32)
    stator = lane >= FACES
    own = [own_ref[row : row + 1, :] for row in (FIRST, SECOND)]
    here = lax.axis_index("blk")
    side = 2 - 2 * lax.rem(here, 2)
    for device, (ref, at_side) in enumerate(
        ((first_ref, side), (own_ref, 1), (second_ref, 2 - side))
    ):
        code = jnp.broadcast_to(ref[CODES : CODES + 1, :], (LANES, LANES)).T
        offset = (2 - at_side) * FACES
        base = jnp.asarray(at_side * FACES, jnp.int32).astype(jnp.float32)
        target = jnp.where(stator, lane - FACES + offset, -1).astype(jnp.float32)
        for h in range(2):
            top = jnp.where(code[h * FACES : (h + 1) * FACES] == target, 1.0, 0.0)
            mine = jnp.where(stator, -1.0, jnp.broadcast_to(own[h], (FACES, LANES)))
            bottom = jnp.where(mine == face + base, 1.0, 0.0)
            columns = slice(h * LANES, (h + 1) * LANES)
            at = device * LANES
            pick[at : at + FACES, columns] = top.astype(jnp.bfloat16)
            pick[at + FACES : at + LANES, columns] = bottom.astype(jnp.bfloat16)


def lift_rows(flow_ref, first_ref, own_ref, second_ref, pick, table_ref, jac_ref, work, coef, emit):
    high, low = split(
        jnp.concatenate([first_ref[...], own_ref[...], second_ref[...]], axis=1)
    )
    matrix = pick[...]
    work[...] = jnp.dot(high, matrix, preferred_element_type=jnp.float32) + jnp.dot(
        low, matrix, preferred_element_type=jnp.float32
    )
    coef[...] = (
        work[ONES : ONES + 1, 0:LANES] * table_ref[72:108, :]
        + work[ONES : ONES + 1, LANES : 2 * LANES] * table_ref[108:144, :]
    )
    axial = flow_ref[2]
    speed = 0.5 * (jnp.abs(axial) + 1.0)
    lane = lax.broadcasted_iota(jnp.int32, (1, LANES), 1)
    scale = (time_step * lift_scale) * jac_ref[:, 0:LANES]
    signed = jnp.where(lane < FACES, scale, -scale)
    damp = speed * scale
    for i in range(NP):
        cross = [
            [table_ref[h * 36 + i * 6 + m : h * 36 + i * 6 + m + 1, :] for m in range(6)]
            for h in range(2)
        ]
        square = [coef[i * 6 + m : i * 6 + m + 1, :] for m in range(6)]
        mean, jump = [], []
        for v in range(NV):
            other = None
            own = None
            for m in range(6):
                rows = pl.ds((v * NP + m) * NP, 6)
                term = cross[0][m] * work[rows, 0:LANES]
                term = term + cross[1][m] * work[rows, LANES : 2 * LANES]
                other = term if other is None else other + term
                term = square[m] * own_ref[rows, :]
                own = term if own is None else own + term
            mean.append(own_ref[pl.ds((v * NP + i) * NP, 6), :] - 0.5 * (own + other))
            jump.append(own - other)
        for v in range(NV):
            flux = axial * mean[v]
            partner = PARTNERS[2].get(v)
            if partner is not None:
                flux = flux + mean[partner]
            emit(v, i, signed * flux - damp * jump[v])


def first_lift_kernel(
    flow_ref, first_ref, own_ref, second_ref, trace_ref, table_ref, jac_ref,
    message_ref, lift_ref, pick, work, coef,
):
    pair_matrix(first_ref, own_ref, second_ref, pick)

    def emit(v, i, value):
        rows = pl.ds((v * NP + i) * NP, 6)
        lift_ref[rows, :] = value
        message_ref[rows, :] = trace_ref[rows, :] + value

    lift_rows(
        flow_ref, first_ref, own_ref, second_ref, pick, table_ref, jac_ref, work, coef, emit
    )
    message_ref[ROWS:MSG, :] = own_ref[ROWS:MSG, :]


def second_lift_kernel(
    flow_ref, first_ref, own_ref, second_ref, pick, table_ref, jac_ref, modes_ref, agg_ref,
    base_hbm, new_hbm, sums_ref, work, coef, lift, block, sems,
):
    faces_in = (slice(None),) * 4 + (pl.ds(0, LANES),)
    fetch = pltpu.make_async_copy(base_hbm.at[faces_in], block, sems.at[0])
    fetch.start()
    aggs = sums_ref.shape[0] * sums_ref.shape[1]
    name = lax.broadcasted_iota(jnp.int32, (aggs, modes_ref.shape[1]), 0)
    member = jnp.where(name == agg_ref[...], 1.0, 0.0).astype(jnp.bfloat16)
    sums = {}

    def emit(v, i, value):
        lift[pl.ds((v * NP + i) * NP, 6), :] = value
        for a in range(2):
            term = COARSE[a][i] * value
            sums[v, a] = term if i == 0 else sums[v, a] + term

    lift_rows(
        flow_ref, first_ref, own_ref, second_ref, pick, table_ref, jac_ref, work, coef, emit
    )
    fetch.wait()
    mask = 0.5 * layer_mask()
    for v in range(NV):
        for i in range(NP):
            for j in range(NP):
                row = (v * NP + i) * NP + j
                block[v, i, j] += mask * jnp.broadcast_to(lift[row : row + 1, :], (NP, LANES))
    store = pltpu.make_async_copy(block, new_hbm.at[faces_in], sems.at[1])
    store.start()
    lane = lax.broadcasted_iota(jnp.int32, (1, LANES), 1)
    jac = jac_ref[:, 0:LANES]
    weight = (0.5 / time_step) / (jac * jac * jac)
    ends = [weight * jnp.where(lane < FACES, COARSE[c][5], COARSE[c][0]) for c in range(2)]
    columns = [column(COARSE[b]) for b in range(2)]
    at = lax.broadcasted_iota(jnp.int32, (8, LANES), 0)
    blocks = []
    for v in range(NV):
        mode = jnp.zeros((8, LANES), jnp.float32)
        for a in range(2):
            for b in range(2):
                total = jnp.sum(columns[b] * sums[v, a], axis=0, keepdims=True)
                for c in range(2):
                    mode = jnp.where(at == a * 4 + b * 2 + c, ends[c] * total, mode)
        blocks.append(mode)
    faces = modes_ref[:, 0:LANES] + jnp.concatenate(blocks, axis=0)
    modes = jnp.concatenate([faces, modes_ref[:, LANES:]], axis=1)
    modes = jnp.concatenate(
        [modes, jnp.zeros((LANES - 8 * NV, modes.shape[1]), jnp.float32)], axis=0
    )
    high, low = split(modes)
    contract = (((1,), (1,)), ((), ()))
    total = lax.dot_general(
        member, high, contract, preferred_element_type=jnp.float32
    ) + lax.dot_general(member, low, contract, preferred_element_type=jnp.float32)
    share = sums_ref.shape[1]
    for s in range(sums_ref.shape[0]):
        sums_ref[s] = total[s * share : (s + 1) * share, :]
    store.wait()


def total_kernel(parts_ref, total_ref):
    total = parts_ref[0]
    for s in range(1, parts_ref.shape[0]):
        total = total + parts_ref[s]
    total_ref[...] = total[:, 0 : total_ref.shape[1]]


def swapped(value, first):
    count = lax.axis_size("blk")
    edges = [(b, (b + 1) % count) for b in range(first, count, 2)]
    return lax.ppermute(value, "blk", edges + [(b, a) for a, b in edges])


def exchanged(value):
    late = swapped(value, 0)
    early = swapped(value, 1)
    return late, early


WHOLE_VMEM = 64800000
VMEM = pl.BlockSpec(memory_space=pltpu.VMEM)
SMEM = pl.BlockSpec(memory_space=pltpu.SMEM)
HBM = pl.BlockSpec(memory_space=pltpu.HBM)


def shape(*dims, dtype=jnp.float32):
    return jax.ShapeDtypeStruct(dims, dtype)


def params(size=48 * 1024 * 1024):
    return pltpu.CompilerParams(vmem_limit_bytes=size)


def local(fields, jacobian, mean_flow, pair_owner, pair_mortar, mortar_proj, coarse_id):
    elements = fields.shape[4]
    spans = lax.axis_size("span")
    aggs = elements * spans // 8
    jac_row = jacobian.reshape(1, elements)
    mats = mortar_proj.reshape(4 * NP * NP)
    dims = (NV, NP, NP, NP, LANES)
    half = pl.BlockSpec(dims, lambda n: (0, 0, 0, 0, n))
    row = pl.BlockSpec((1, LANES), lambda n: (0, n))
    whole = pl.BlockSpec((MSG, LANES), lambda n: (0, 0))
    fixed = lambda *d: pl.BlockSpec(d, lambda n: (0,) * len(d))
    tiles = pltpu.VMEM((NV * NP * NP * 8, LANES), jnp.float32)
    grid = (elements // LANES,)
    volume_cost = pl.CostEstimate(
        flops=120 * NV * 216 * elements, bytes_accessed=3 * 4 * 1440 * elements, transcendentals=0
    )

    message = pl.pallas_call(
        message_kernel,
        in_specs=[HBM] * 3,
        out_specs=VMEM,
        out_shape=shape(MSG, LANES),
        scratch_shapes=[
            pltpu.VMEM(dims, jnp.float32),
            pltpu.VMEM((1, LANES), jnp.int32),
            pltpu.VMEM((1, LANES), jnp.int32),
            pltpu.SemaphoreType.DMA((3,)),
        ],
        compiler_params=params(WHOLE_VMEM),
        name="face_message",
    )(fields, pair_owner.reshape(1, LANES), pair_mortar.reshape(1, LANES))
    first, second = exchanged(message)

    rate, trace, table = pl.pallas_call(
        first_volume_kernel,
        grid=grid,
        in_specs=[SMEM, SMEM, half, row],
        out_specs=[half, whole, fixed(144, LANES)],
        out_shape=[shape(*fields.shape), shape(MSG, LANES), shape(144, LANES)],
        scratch_shapes=[tiles, tiles],
        compiler_params=params(),
        cost_estimate=volume_cost,
        name="first_volume",
    )(mean_flow, mats, fields, jac_row)

    message2, lift, pick = pl.pallas_call(
        first_lift_kernel,
        in_specs=[SMEM] + [VMEM] * 6,
        out_specs=[VMEM] * 3,
        out_shape=[
            shape(MSG, LANES),
            shape(ROWS, LANES),
            shape(3 * LANES, 2 * LANES, dtype=jnp.bfloat16),
        ],
        scratch_shapes=[
            pltpu.VMEM((MSG, 2 * LANES), jnp.float32),
            pltpu.VMEM((36, LANES), jnp.float32),
        ],
        compiler_params=params(),
        name="first_lift",
    )(mean_flow, first, message, second, trace, table, jac_row)
    first2, second2 = exchanged(message2)

    base, modes = pl.pallas_call(
        second_volume_kernel,
        grid=grid,
        in_specs=[SMEM, half, row, half, fixed(ROWS, LANES)],
        out_specs=[half, pl.BlockSpec((8 * NV, LANES), lambda n: (0, n))],
        out_shape=[shape(*fields.shape), shape(8 * NV, elements)],
        scratch_shapes=[tiles, tiles],
        compiler_params=params(),
        cost_estimate=volume_cost,
        name="second_volume",
    )(mean_flow, fields, jac_row, rate, lift)

    new_fields, sums = pl.pallas_call(
        second_lift_kernel,
        in_specs=[SMEM] + [VMEM] * 8 + [HBM],
        out_specs=[HBM, VMEM],
        out_shape=[shape(*fields.shape), shape(spans, aggs // spans, LANES)],
        scratch_shapes=[
            pltpu.VMEM((MSG, 2 * LANES), jnp.float32),
            pltpu.VMEM((36, LANES), jnp.float32),
            pltpu.VMEM((ROWS, LANES), jnp.float32),
            pltpu.VMEM(dims, jnp.float32),
            pltpu.SemaphoreType.DMA((2,)),
        ],
        input_output_aliases={9: 0},
        compiler_params=params(),
        name="second_lift",
    )(
        mean_flow, first2, message2, second2, pick, table, jac_row, modes,
        coarse_id.reshape(1, elements), base,
    )
    parts = lax.all_to_all(sums, "span", 0, 0)
    coarse = jnp.sum(parts, axis=0)[:, : 8 * NV]
    return new_fields, coarse.T


def solution(mesh):
    return jax.shard_map(
        local,
        mesh=mesh,
        in_specs=(
            P(None, None, None, None, ("blk", "span")),
            P(("blk", "span")),
            P(),
            P(("blk", "span"), None),
            P(("blk", "span")),
            P(),
            P(("blk", "span")),
        ),
        out_specs=(P(None, None, None, None, ("blk", "span")), P(None, ("blk", "span"))),
        check_vma=False,
    )
```
